128 devices in a mesh: fine: 32 (over z, x, core), sub: 4 (over y).
Axes of the slice: x: 4, y: 4, z: 4, core: 2. Of those that a mesh axis runs over, the one named last changes fastest.
Arguments:
- a_tiles: bfloat16 [4096, 8, 128, 128], P(('fine', 'sub')), may hold values from -5 to 5
- a_cols: int32 [4096, 8], P(('fine', 'sub')), may hold values from 0 to 4095, as said below
- a_count: int32 [4096], P(('fine', 'sub')), may hold values from 2 to 8
- p_tiles: bfloat16 [4096, 4, 128, 128], P(('fine', 'sub')), may hold values from -0.25 to 0.25
- p_cols: int32 [4096, 4], P(('fine', 'sub')), may hold values from 0 to 255, as said below
Outputs:
- coarse_op: float32 [256, 7, 128, 128], P('fine', None, 'sub')
The draws below stay inside these ranges and needn't reach their ends.
Inputs may be any that keep to these rules, and one draw needn't show every extreme that they name: `a_cols`: each entry is within 16 of its row's index; slot 0 of every row is the row itself. `p_cols`: each entry is within one of its row's index divided by 16, rounded down.
All inputs are finite; a program needn't handle non-finite values.
Results may differ from the reference program's by a relative error of at most 0.0065.
Values may be sent and summed in bfloat16 or wider, within the bound.
No kernel may reach another device: no remote copies, remote signals or barrier semaphores. Data moves between devices by JAX's collectives and lax.ppermute only.
A program may use at most 128 MiB of HBM per device.

```python
import jax
import jax.numpy as jnp
from jax import lax

TILE = 128
A_SLOTS = 8
P_SLOTS = 4
AGG_RATIO = 16
REACH = 16
ROWS_DEV = 32
FINE_ROWS = 4096
COARSE_ROWS = 256


def draw_a_cols(key, part):
    key = jax.random.fold_in(key, 11)
    row_ids = jnp.arange(FINE_ROWS, dtype=jnp.int32)[:, None]
    slot_ids = jnp.arange(A_SLOTS, dtype=jnp.int32)[None, :]
    jumps = jax.random.randint(key, (FINE_ROWS, A_SLOTS), -REACH, REACH + 1, dtype=jnp.int32)
    position = row_ids % ROWS_DEV
    jumps = jnp.where(slot_ids == 0, 0, jumps)
    jumps = jnp.where((slot_ids == 1) & (position == 0), -REACH, jumps)
    jumps = jnp.where((slot_ids == 1) & (position == ROWS_DEV - 1), REACH, jumps)
    return jnp.clip(row_ids + jumps, 0, FINE_ROWS - 1)


def draw_a_count(key, part):
    key = jax.random.fold_in(key, 23)
    counts = jax.random.randint(key, (FINE_ROWS,), 2, A_SLOTS + 1, dtype=jnp.int32)
    position = jnp.arange(FINE_ROWS, dtype=jnp.int32) % ROWS_DEV
    counts = jnp.where(position == 0, A_SLOTS, counts)
    counts = jnp.where(position == 1, 2, counts)
    return counts


def draw_p_cols(key, part):
    key = jax.random.fold_in(key, 37)
    row_ids = jnp.arange(FINE_ROWS, dtype=jnp.int32)[:, None]
    slot_ids = jnp.arange(P_SLOTS, dtype=jnp.int32)[None, :]
    jumps = jax.random.randint(key, (FINE_ROWS, P_SLOTS), -1, 2, dtype=jnp.int32)
    jumps = jnp.where((slot_ids == 0) & (row_ids == 0), -1, jumps)
    jumps = jnp.where((slot_ids == 0) & (row_ids == FINE_ROWS - 1), 1, jumps)
    return jnp.clip(row_ids // AGG_RATIO + jumps, 0, COARSE_ROWS - 1)


def block_levels(rng, dims, split, least, largest):
    def one(axis_at, parts):
        steps = jax.random.uniform(jax.random.fold_in(jax.random.fold_in(rng, 6), axis_at), (parts,), jnp.float32, least / len(split), largest / len(split))
        return jnp.repeat(jnp.exp(steps), dims[axis_at] // parts).reshape((-1,) + (1,) * (len(dims) - axis_at - 1))

    gain = one(*split[0])
    for cut in split[1:]:
        gain = gain * one(*cut)
    return gain


def noise(stream_key, extent, spread, most, pieces=(), held_as=jnp.bfloat16):
    drawn = jax.random.normal(stream_key, extent, jnp.float32) * spread
    if len(pieces) > 0:
        drawn = block_levels(stream_key, extent, pieces, -0.22, 0.18) * drawn
    return jnp.clip(drawn, min=-most, max=most).astype(held_as)


def setup_inputs(seed: int = 0) -> dict:
    streams_of = jax.random.split(jax.random.key(seed), 6)
    return {
        "a_tiles": noise(streams_of[0], (FINE_ROWS, A_SLOTS, TILE, TILE), (A_SLOTS ** -0.5), 5.0, ((0, 128),)),
        "a_cols": draw_a_cols(jax.random.fold_in(streams_of[5], 71), 0),
        "a_count": draw_a_count(jax.random.fold_in(streams_of[5], 71), 0),
        "p_tiles": noise(streams_of[3], (FINE_ROWS, P_SLOTS, TILE, TILE), (P_SLOTS * TILE) ** -0.5, 0.25, ((0, 128),)),
        "p_cols": draw_p_cols(jax.random.fold_in(streams_of[5], 71), 0),
    }


def reference(a_tiles, a_cols, a_count, p_tiles, p_cols):
    fine_total = a_tiles.shape[0]
    block_rows = 8 if fine_total % 8 == 0 else fine_total
    window_rows = (block_rows - 1) // AGG_RATIO + 3
    slot_index = jnp.arange(A_SLOTS, dtype=jnp.int32)
    offset_index = jnp.arange(5, dtype=jnp.int32)
    window_index = jnp.arange(window_rows, dtype=jnp.int32)
    band_index = jnp.arange(7, dtype=jnp.int32)
    highest = lax.Precision.HIGHEST

    def step(total, start):
        row_ids = start + jnp.arange(block_rows, dtype=jnp.int32)
        a_block = lax.dynamic_slice_in_dim(a_tiles, start, block_rows, 0).astype(jnp.float32)
        col_block = lax.dynamic_slice_in_dim(a_cols, start, block_rows, 0)
        used = lax.dynamic_slice_in_dim(a_count, start, block_rows, 0)
        own_tiles = lax.dynamic_slice_in_dim(p_tiles, start, block_rows, 0).astype(jnp.float32)
        own_cols = lax.dynamic_slice_in_dim(p_cols, start, block_rows, 0)
        agg_rows = row_ids // AGG_RATIO
        fetched = p_tiles[col_block].astype(jnp.float32)
        fetched_cols = p_cols[col_block]
        valid = slot_index[None, :] < used[:, None]
        products = jnp.einsum("gkab,gkmbc->gkmac", a_block, fetched, precision=highest)
        rel_cols = fetched_cols - agg_rows[:, None, None] + 2
        picker = ((rel_cols[..., None] == offset_index) & valid[:, :, None, None]).astype(jnp.float32)
        ap_rows = jnp.einsum("gkmo,gkmac->goac", picker, products, precision=highest)
        ap_rows = lax.optimization_barrier(ap_rows.astype(jnp.bfloat16)).astype(jnp.float32)
        restricted = jnp.einsum("gmba,gobc->gmoac", own_tiles, ap_rows, precision=highest)
        coarse_base = agg_rows[0] - 1
        row_rel = own_cols - coarse_base
        shift_rel = own_cols - agg_rows[:, None]
        band_rel = offset_index[None, None, :] + 1 - shift_rel[:, :, None]
        row_pick = (row_rel[..., None] == window_index).astype(jnp.float32)
        band_pick = (band_rel[..., None] == band_index).astype(jnp.float32)
        weights = row_pick[:, :, None, :, None] * band_pick[:, :, :, None, :]
        contrib = jnp.einsum("gmoij,gmoac->ijac", weights, restricted, precision=highest)
        current = lax.dynamic_slice_in_dim(total, coarse_base + 1, window_rows, 0)
        total = lax.dynamic_update_slice_in_dim(total, current + contrib, coarse_base + 1, 0)
        return total, None

    initial = jnp.zeros((COARSE_ROWS + window_rows + 2, 7, TILE, TILE), jnp.float32)
    starts = jnp.arange(0, fine_total, block_rows, dtype=jnp.int32)
    total, unused = lax.scan(step, initial, starts)
    return total[1:COARSE_ROWS + 1]
```

```python
import jax
import jax.numpy as jnp
from jax import lax
from jax.experimental import pallas as pl
from jax.experimental.pallas import tpu as pltpu
from jax.sharding import PartitionSpec as P

AGG = 16
TILE = 128
SLOTS_A = 8
SLOTS_P = 4
ROWS = 32
SUBS = 4
F32 = jnp.float32
BF16 = jnp.bfloat16
MIB = 1 << 20


def place():
    fine = lax.axis_index("fine")
    sub = lax.axis_index("sub")
    return fine * SUBS + sub, sub, lax.rem(sub, 2)


def collapse_kernel(cols, p_ref, pc_ref, *sent):
    step = pl.program_id(0)
    steps = pl.num_programs(0)
    rows = p_ref.shape[0]
    device, sub, parity = place()
    half = step // (steps // 2)
    agg = device * 2 + half
    by_b = half ^ (1 - parity)
    for r in range(rows):
        row = step * rows + r
        local = row - half * AGG
        tiles = [p_ref[r, k].astype(F32) for k in range(SLOTS_P)]
        rel = [cols[row, k] - agg for k in range(SLOTS_P)]
        for c in range(3):
            m = jnp.where(half == 1, 1 - c, c - 1)
            value = jnp.where(rel[0] == m, tiles[0], 0.0)
            for k in range(1, SLOTS_P):
                value = value + jnp.where(rel[k] == m, tiles[k], 0.0)
            value = value.astype(BF16)
            pc_ref[m + 1, r] = value

            @pl.when(by_b == 0)
            def _():
                sent[c][local] = value

            @pl.when(by_b == 1)
            def _():
                sent[3 + c][local] = value


def collapse(p_tiles, p_cols):
    rows = 4
    message = jax.ShapeDtypeStruct((AGG, TILE, TILE), BF16)
    whole = pl.BlockSpec((AGG, TILE, TILE), lambda i, *_: (0, 0, 0))
    return pl.pallas_call(
        collapse_kernel,
        out_shape=[jax.ShapeDtypeStruct((3, ROWS, TILE, TILE), BF16)] + [message] * 6,
        grid_spec=pltpu.PrefetchScalarGridSpec(
            num_scalar_prefetch=1,
            grid=(ROWS // rows,),
            in_specs=[pl.BlockSpec((rows, SLOTS_P, TILE, TILE), lambda i, *_: (i, 0, 0, 0))],
            out_specs=[pl.BlockSpec((3, rows, TILE, TILE), lambda i, *_: (0, i, 0, 0))]
            + [whole] * 6,
        ),
        compiler_params=pltpu.CompilerParams(vmem_limit_bytes=24 * MIB),
        cost_estimate=pl.CostEstimate(flops=12 * MIB, bytes_accessed=10 * MIB, transcendentals=0),
    )(p_cols, p_tiles)


def local_kernel(acols, acount, a_ref, pc_ref, out_ref, rh_ref, total):
    step = pl.program_id(0)
    steps = pl.num_programs(0)
    rows = a_ref.shape[0]
    device, sub, parity = place()
    half = step // (steps // 2)
    inner = lax.rem(step, steps // 2)
    base = device * ROWS + half * AGG - AGG

    @pl.when(inner == 0)
    def _():
        def clear(i, carry):
            total[i] = jnp.zeros((3 * TILE, TILE), F32)
            return carry

        lax.fori_loop(0, 3 * AGG, clear, 0)

    for r in range(rows):
        row = step * rows + r
        own = jnp.concatenate([pc_ref[m, row].T for m in range(3)], axis=0)
        used = acount[row]
        for k in range(0, SLOTS_A, 2):
            pair = jnp.concatenate([a_ref[r, k], a_ref[r, k + 1]], axis=1)
            both = jnp.dot(own, pair, preferred_element_type=F32)
            for e in range(2):
                at = jnp.where(k + e < used, acols[row, k + e] - base, 3 * AGG)
                total[at] += both[:, e * TILE : (e + 1) * TILE]

    @pl.when(inner == steps // 2 - 1)
    def _():
        for c in range(AGG):
            rh_ref[0, :, c * TILE : (c + 1) * TILE] = total[32 * half + c].astype(BF16)
        out_ref[...] = jnp.zeros_like(out_ref)
        for b in range(2):
            first = AGG * (b - half + 1)
            left = jnp.concatenate([total[first + c].astype(BF16) for c in range(AGG)], axis=1)
            right = jnp.concatenate(
                [pc_ref[m, AGG * b : AGG * (b + 1)].reshape(AGG * TILE, TILE) for m in range(3)],
                axis=1,
            )
            part = jnp.dot(left, right, preferred_element_type=F32)
            for m in range(3):
                out_ref[0, b - half + 1 + m] += part[:, m * TILE : (m + 1) * TILE]


def local_part(a_tiles, a_cols, a_count, pc):
    rows = 4
    half_steps = ROWS // rows // 2
    return pl.pallas_call(
        local_kernel,
        out_shape=[
            jax.ShapeDtypeStruct((2, 5, 3 * TILE, TILE), F32),
            jax.ShapeDtypeStruct((2, 3 * TILE, AGG * TILE), BF16),
        ],
        grid_spec=pltpu.PrefetchScalarGridSpec(
            num_scalar_prefetch=2,
            grid=(ROWS // rows,),
            in_specs=[
                pl.BlockSpec((rows, SLOTS_A, TILE, TILE), lambda i, *_: (i, 0, 0, 0)),
                pl.BlockSpec((3, ROWS, TILE, TILE), lambda i, *_: (0, 0, 0, 0)),
            ],
            out_specs=[
                pl.BlockSpec((1, 5, 3 * TILE, TILE), lambda i, *_: (i // half_steps, 0, 0, 0)),
                pl.BlockSpec((1, 3 * TILE, AGG * TILE), lambda i, *_: (i // half_steps, 0, 0)),
            ],
            scratch_shapes=[pltpu.VMEM((3 * AGG + 1, 3 * TILE, TILE), F32)],
        ),
        compiler_params=pltpu.CompilerParams(vmem_limit_bytes=44 * MIB),
        cost_estimate=pl.CostEstimate(
            flops=8 * 1024 * MIB, bytes_accessed=16 * MIB, transcendentals=0
        ),
    )(a_cols, a_count, a_tiles, pc)


def finish_kernel(chunk, ha_ref, hb_ref, rh_ref, out_ref, mine, to1, to2, to3, tiles):
    device, sub, parity = place()
    count = tiles.shape[1]
    for x, halo in enumerate((ha_ref, hb_ref)):
        side = x ^ (1 - parity)
        part = jnp.dot(
            rh_ref[side], halo[...].reshape(AGG * TILE, TILE), preferred_element_type=F32
        )
        part = part + out_ref[side, jnp.where(side == 0, 2 - chunk, 2 + chunk)]
        if chunk < 2:
            other = out_ref[1 - side, jnp.where(side == 0, 1 - chunk, 3 + chunk)]
            low = jnp.where(side == 0, part, other)
            high = jnp.where(side == 0, other, part)
            tiles[side, 0] = low[:TILE]
            tiles[side, 1] = low[TILE : 2 * TILE] + high[:TILE]
            tiles[side, 2] = low[2 * TILE :] + high[TILE : 2 * TILE]
            tiles[side, 3] = high[2 * TILE :]
        else:
            for t in range(3):
                tiles[side, t] = part[t * TILE : (t + 1) * TILE]
    wide = TILE // SUBS
    for d, target in enumerate((mine, to1, to2, to3)):
        rows = pl.ds(pl.multiple_of((sub ^ d) * wide, wide), wide)
        for side in range(2):
            for i in range(count):
                target[side, i] = tiles[side, i, rows, :].astype(target.dtype)


def finish_chunk(chunk, ha, hb, rh, local):
    count = 4 if chunk < 2 else 3
    shape = (2, count, TILE // SUBS, TILE)

    def kernel(*refs):
        finish_kernel(chunk, *refs)

    return pl.pallas_call(
        kernel,
        out_shape=[jax.ShapeDtypeStruct(shape, F32)] + [jax.ShapeDtypeStruct(shape, BF16)] * 3,
        in_specs=[pl.BlockSpec(memory_space=pltpu.VMEM)] * 4,
        out_specs=[pl.BlockSpec(memory_space=pltpu.VMEM)] * 4,
        scratch_shapes=[pltpu.VMEM((2, count, TILE, TILE), F32)],
        compiler_params=pltpu.CompilerParams(vmem_limit_bytes=24 * MIB),
        cost_estimate=pl.CostEstimate(
            flops=400 * MIB, bytes_accessed=6 * MIB, transcendentals=0
        ),
    )(ha, hb, rh, local)


def gather_kernel(*refs):
    parts, (out_ref, below_ref, above_ref, window) = refs[:12], refs[12:]
    device, sub, parity = place()
    window[...] = jnp.zeros_like(window)
    for chunk in range(3):
        for d in range(4):
            part = parts[chunk * 4 + d]
            first = 2 * (sub ^ d)
            for side in range(2):
                column = 1 + chunk if side else -chunk
                for t in range(part.shape[1]):
                    i = t if chunk < 2 else t + side
                    if 0 <= column - i + 4 < 7:
                        window[first + i, column - i + 4] += part[side, t].astype(F32)
    out_ref[...] = window[1:9]
    below_ref[...] = window[0].astype(BF16)
    above_ref[...] = window[9].astype(BF16)


def gather_parts(parts):
    wide = TILE // SUBS
    edge = jax.ShapeDtypeStruct((7, wide, TILE), BF16)
    return pl.pallas_call(
        gather_kernel,
        out_shape=[jax.ShapeDtypeStruct((8, 7, wide, TILE), F32), edge, edge],
        in_specs=[pl.BlockSpec(memory_space=pltpu.VMEM)] * 12,
        out_specs=[pl.BlockSpec(memory_space=pltpu.VMEM)] * 3,
        scratch_shapes=[pltpu.VMEM((10, 7, wide, TILE), F32)],
        compiler_params=pltpu.CompilerParams(vmem_limit_bytes=16 * MIB),
    )(*parts)


def edge_kernel(from_below, from_above, whole_ref, out_ref):
    out_ref[...] = whole_ref[...]
    out_ref[0] += from_below[...].astype(F32)
    out_ref[7] += from_above[...].astype(F32)


def add_edges(from_below, from_above, whole):
    return pl.pallas_call(
        edge_kernel,
        out_shape=jax.ShapeDtypeStruct(whole.shape, F32),
        in_specs=[pl.BlockSpec(memory_space=pltpu.VMEM)] * 3,
        out_specs=pl.BlockSpec(memory_space=pltpu.VMEM),
        compiler_params=pltpu.CompilerParams(vmem_limit_bytes=16 * MIB),
    )(from_below, from_above, whole)


def shards(a_tiles, a_cols, a_count, p_tiles, p_cols):
    fines = lax.axis_size("fine")
    total = fines * SUBS
    pc, *sent = collapse(p_tiles, p_cols)
    pairs_a = [(i, i ^ 1) for i in range(total)]
    pairs_b = [(i, i + 1) for i in range(1, total - 1, 2)]
    pairs_b = pairs_b + [(b, a) for a, b in pairs_b]
    both = ("fine", "sub")
    halo = []
    for c in range(3):
        halo.append(
            (lax.ppermute(sent[c], both, pairs_a), lax.ppermute(sent[3 + c], both, pairs_b))
        )
    local, rh = local_part(a_tiles, a_cols, a_count, pc)
    parts = []
    for c in range(3):
        mine, *out = finish_chunk(c, halo[c][0], halo[c][1], rh, local)
        parts.append(mine)
        for d in range(3):
            route = [(i, i ^ (d + 1)) for i in range(SUBS)]
            parts.append(lax.ppermute(out[d], "sub", route))
    whole, below, above = gather_parts(parts)
    from_above = lax.ppermute(below, "fine", [(i + 1, i) for i in range(fines - 1)])
    from_below = lax.ppermute(above, "fine", [(i, i + 1) for i in range(fines - 1)])
    return add_edges(from_below, from_above, whole)


def solution(mesh):
    in_specs = (
        P(("fine", "sub"), None, None, None),
        P(("fine", "sub"), None),
        P(("fine", "sub")),
        P(("fine", "sub"), None, None, None),
        P(("fine", "sub"), None),
    )
    out_specs = P("fine", None, "sub", None)
    return jax.shard_map(shards, mesh=mesh, in_specs=in_specs, out_specs=out_specs, check_vma=False)
```

```python
import jax
import jax.numpy as jnp
from jax import lax
from jax.experimental import pallas as pl
from jax.experimental.pallas import tpu as pltpu
from jax.sharding import PartitionSpec as P

AGG = 16
TILE = 128
SLOTS_A = 8
SLOTS_P = 4
ROWS = 32
SUBS = 4
WIDE = TILE // SUBS
F32 = jnp.float32
BF16 = jnp.bfloat16
MIB = 1 << 20
STEP = 4
GROUPS = ((0, 1), (2,))
VMEM = pl.BlockSpec(memory_space=pltpu.VMEM)
SMEM = pl.BlockSpec(memory_space=pltpu.SMEM)
HBM = pl.BlockSpec(memory_space=pltpu.HBM)


def place():
    fine = lax.axis_index("fine")
    sub = lax.axis_index("sub")
    return fine * SUBS + sub, sub, lax.rem(sub, 2)


def where_of(chunk):
    for g, group in enumerate(GROUPS):
        if chunk in group:
            return g, group.index(chunk)
    raise ValueError(chunk)


def fetch(source, target, sems, first, i):
    rows = pl.ds((first + i) * STEP, STEP)
    here = pl.ds(i * STEP, STEP)
    return pltpu.make_async_copy(source.at[rows], target.at[here], sems.at[i])


def collapse_rows(group, cols, p_hbm, held, sems, by_a, by_b, half):
    device, sub, parity = place()
    agg = device * 2 + half
    steps = AGG // STEP
    part = TILE // 4

    def fill(target):
        def rows_at(i, carry):
            first = half * steps + i
            fetch(p_hbm, held, sems, 0, first).wait()
            for r in range(STEP):
                row = first * STEP + r
                rel = [cols[k, row] - agg for k in range(SLOTS_P)]
                for q in range(4):
                    lines = slice(q * part, (q + 1) * part)
                    tiles = [held[row, k, lines].astype(F32) for k in range(SLOTS_P)]
                    for at, c in enumerate(group):
                        m = 1 - c if half == 1 else c - 1
                        value = jnp.where(rel[0] == m, tiles[0], 0.0)
                        for k in range(1, SLOTS_P):
                            value = value + jnp.where(rel[k] == m, tiles[k], 0.0)
                        target[at, i * STEP + r, lines] = value.astype(BF16)
            return carry

        lax.fori_loop(0, steps, rows_at, 0)

    @pl.when(parity == 1 - half)
    def _():
        fill(by_a)

    @pl.when(parity == half)
    def _():
        fill(by_b)


def collapse_kernel(cols, p_hbm, by_a, by_b, held, sems):
    for i in range(ROWS // STEP):
        fetch(p_hbm, held, sems, 0, i).start()
    for half in range(2):
        collapse_rows(GROUPS[0], cols, p_hbm, held, sems, by_a, by_b, half)


def collapse(p_tiles, p_cols):
    shape = jax.ShapeDtypeStruct((len(GROUPS[0]), AGG, TILE, TILE), BF16)
    return pl.pallas_call(
        collapse_kernel,
        out_shape=[shape, shape],
        in_specs=[SMEM, HBM],
        out_specs=[VMEM] * 2,
        scratch_shapes=[
            pltpu.VMEM((ROWS, SLOTS_P, TILE, TILE), BF16),
            pltpu.SemaphoreType.DMA((ROWS // STEP,)),
        ],
        compiler_params=pltpu.CompilerParams(vmem_limit_bytes=48 * MIB),
        cost_estimate=pl.CostEstimate(flops=8 * MIB, bytes_accessed=6 * MIB, transcendentals=0),
    )(p_cols.T, p_tiles)


def local_rows(half, acols, acount, a_hbm, by_a, by_b, out_ref, rh_ref, total, held, pc, sems):
    device, sub, parity = place()
    base = device * ROWS + half * AGG - AGG

    def spread(i, carry):
        for c in range(3):
            g, at = where_of(c)

            @pl.when(parity == 0)
            def _():
                pc[2 - c, AGG + i] = by_a[g][at, i]
                pc[c, i] = by_b[g][at, i]

            @pl.when(parity == 1)
            def _():
                pc[c, i] = by_a[g][at, i]
                pc[2 - c, AGG + i] = by_b[g][at, i]

        total[3 * i] = jnp.zeros((3 * TILE, TILE), F32)
        total[3 * i + 1] = jnp.zeros((3 * TILE, TILE), F32)
        total[3 * i + 2] = jnp.zeros((3 * TILE, TILE), F32)
        return carry

    lax.fori_loop(0, AGG, spread, 0)

    def rows_at(i, carry):
        fetch(a_hbm, held, sems, half * (AGG // STEP), i).wait()
        for r in range(STEP):
            near = i * STEP + r
            row = half * AGG + near
            own = jnp.concatenate([pc[m, row].T for m in range(3)], axis=0)
            used = acount[row]
            for k in range(0, SLOTS_A, 2):
                pair = jnp.concatenate([held[near, k], held[near, k + 1]], axis=1)
                both = jnp.dot(own, pair, preferred_element_type=F32)
                for e in range(2):
                    at = jnp.where(k + e < used, acols[k + e, row] - base, 3 * AGG)
                    total[at] += both[:, e * TILE : (e + 1) * TILE]
        return carry

    lax.fori_loop(0, AGG // STEP, rows_at, 0)
    for c in range(AGG):
        rh_ref[half, :, c * TILE : (c + 1) * TILE] = total[2 * AGG * half + c].astype(BF16)
    for o in range(5):
        out_ref[half, o] = jnp.zeros((3 * TILE, TILE), F32)
    for b in range(2):
        first = AGG * (b - half + 1)
        left = jnp.concatenate([total[first + c].astype(BF16) for c in range(AGG)], axis=1)
        right = jnp.concatenate(
            [pc[m, AGG * b : AGG * (b + 1)].reshape(AGG * TILE, TILE) for m in range(3)],
            axis=1,
        )
        part = jnp.dot(left, right, preferred_element_type=F32)
        for m in range(3):
            out_ref[half, b - half + 1 + m] += part[:, m * TILE : (m + 1) * TILE]


def first_kernel(
    acols, acount, cols, a_hbm, p_hbm, a0, b0, a1, b1, out_ref, rh_ref, total, held, pc, p_held, sems, p_sems
):
    for i in range(ROWS // STEP):
        fetch(p_hbm, p_held, p_sems, 0, i).start()
    for i in range(AGG // STEP):
        fetch(a_hbm, held, sems, 0, i).start()
    for half in range(2):
        collapse_rows(GROUPS[1], cols, p_hbm, p_held, p_sems, a1, b1, half)
    local_rows(
        0, acols, acount, a_hbm, (a0, a1), (b0, b1), out_ref, rh_ref, total, held, pc, sems
    )


def second_kernel(
    acols, acount, a_hbm, a0, b0, a1, b1, out_in, rh_in, out_ref, rh_ref, total, held, pc, sems
):
    for i in range(AGG // STEP):
        fetch(a_hbm, held, sems, AGG // STEP, i).start()
    local_rows(
        1, acols, acount, a_hbm, (a0, a1), (b0, b1), out_ref, rh_ref, total, held, pc, sems
    )


LOCAL = [
    jax.ShapeDtypeStruct((2, 5, 3 * TILE, TILE), F32),
    jax.ShapeDtypeStruct((2, 3 * TILE, AGG * TILE), BF16),
]


def scratch():
    return [
        pltpu.VMEM((3 * AGG + 1, 3 * TILE, TILE), F32),
        pltpu.VMEM((AGG, SLOTS_A, TILE, TILE), BF16),
        pltpu.VMEM((3, ROWS, TILE, TILE), BF16),
    ]


def first_half(a_tiles, a_cols, a_count, p_tiles, p_cols, a0, b0):
    shape = jax.ShapeDtypeStruct((len(GROUPS[1]), AGG, TILE, TILE), BF16)
    return pl.pallas_call(
        first_kernel,
        out_shape=[shape, shape] + LOCAL,
        in_specs=[SMEM, SMEM, SMEM, HBM, HBM, VMEM, VMEM],
        out_specs=[VMEM] * 4,
        scratch_shapes=scratch()
        + [
            pltpu.VMEM((ROWS, SLOTS_P, TILE, TILE), BF16),
            pltpu.SemaphoreType.DMA((AGG // STEP,)),
            pltpu.SemaphoreType.DMA((ROWS // STEP,)),
        ],
        compiler_params=pltpu.CompilerParams(vmem_limit_bytes=40 * MIB),
        cost_estimate=pl.CostEstimate(
            flops=8 * 1024 * MIB, bytes_accessed=8 * MIB, transcendentals=0
        ),
    )(a_cols.T, a_count, p_cols.T, a_tiles, p_tiles, a0, b0)


def second_half(a_tiles, a_cols, a_count, a0, b0, a1, b1, local, rh):
    return pl.pallas_call(
        second_kernel,
        out_shape=LOCAL,
        in_specs=[SMEM, SMEM, HBM] + [VMEM] * 6,
        out_specs=[VMEM] * 2,
        scratch_shapes=scratch() + [pltpu.SemaphoreType.DMA((AGG // STEP,))],
        input_output_aliases={7: 0, 8: 1},
        compiler_params=pltpu.CompilerParams(vmem_limit_bytes=40 * MIB),
        cost_estimate=pl.CostEstimate(
            flops=8 * 1024 * MIB, bytes_accessed=8 * MIB, transcendentals=0
        ),
    )(a_cols.T, a_count, a_tiles, a0, b0, a1, b1, local, rh)


def tiles_of(chunk):
    return (0, 1, 2, 3) if chunk < 2 else (0, 1, 2)


def edge_tiles(group):
    below, above, at = [], [], 0
    for chunk in group:
        for t in tiles_of(chunk):
            for side in range(2):
                i = t if chunk < 2 else t + side
                column = 1 + chunk if side else -chunk
                if i == 0:
                    below.append((side, at, column + 4))
                if i == 3:
                    above.append((side, at, column + 1))
            at += 1
    below = [b for b in below if 2 <= b[2] < 7]
    above = [b for b in above if 0 <= b[2] < 5]
    return sorted(below, key=lambda b: b[2]), sorted(above, key=lambda b: b[2])


def finish_kernel(group, ha_ref, hb_ref, rh_ref, out_ref, *refs):
    tiles, edge = refs[-2:]
    device, sub, parity = place()
    for x, halo in enumerate((ha_ref, hb_ref)):
        side = x ^ (1 - parity)
        right = jnp.concatenate(
            [halo[at].reshape(AGG * TILE, TILE) for at in range(len(group))], axis=1
        )
        parts = jnp.dot(rh_ref[side], right, preferred_element_type=F32)
        first = 0
        for at, chunk in enumerate(group):
            part = parts[:, at * TILE : (at + 1) * TILE]
            part = part + out_ref[side, jnp.where(side == 0, 2 - chunk, 2 + chunk)]
            if chunk < 2:
                other = out_ref[1 - side, jnp.where(side == 0, 1 - chunk, 3 + chunk)]
                low = jnp.where(side == 0, part, other)
                high = jnp.where(side == 0, other, part)
                tiles[side, first] = low[:TILE]
                tiles[side, first + 1] = low[TILE : 2 * TILE] + high[:TILE]
                tiles[side, first + 2] = low[2 * TILE :] + high[TILE : 2 * TILE]
                tiles[side, first + 3] = high[2 * TILE :]
            else:
                for t in range(3):
                    tiles[side, first + t] = part[t * TILE : (t + 1) * TILE]
            first += len(tiles_of(chunk))
    below, above = edge_tiles(group)
    taken = edge.shape[0] - len(below)
    if taken:
        edge[:taken] = refs[0][...]

    @pl.when(sub == 0)
    def _():
        for n, (side, at, _j) in enumerate(below):
            edge[taken + n] = tiles[side, at].astype(BF16)

    @pl.when(sub == SUBS - 1)
    def _():
        for n, (side, at, _j) in enumerate(above):
            edge[taken + n] = tiles[side, at].astype(BF16)


def finish(group, ha, hb, rh, local, *before):
    count = sum(len(tiles_of(c)) for c in group)
    edges = len(edge_tiles(group)[0]) + sum(b.shape[0] for b in before)

    def kernel(*refs):
        finish_kernel(group, *refs)

    return pl.pallas_call(
        kernel,
        out_shape=[
            jax.ShapeDtypeStruct((2, count, TILE, TILE), F32),
            jax.ShapeDtypeStruct((edges, TILE, TILE), BF16),
        ],
        in_specs=[VMEM] * (4 + len(before)),
        out_specs=[VMEM] * 2,
        compiler_params=pltpu.CompilerParams(vmem_limit_bytes=24 * MIB),
        cost_estimate=pl.CostEstimate(
            flops=400 * MIB, bytes_accessed=6 * MIB, transcendentals=0
        ),
    )(ha, hb, rh, local, *before)


def split_kernel(tiles0, tiles1, edge, mine, to1, to2, to3):
    device, sub, parity = place()
    for d, target in enumerate((mine, to1, to2, to3)):
        rows = pl.ds(pl.multiple_of((sub ^ d) * WIDE, WIDE), WIDE)
        base, taken = 0, 0
        for group, tiles in zip(GROUPS, (tiles0, tiles1), strict=True):
            below, above = edge_tiles(group)
            for side in range(2):
                for i in range(tiles.shape[1]):
                    target[side, base + i] = tiles[side, i, rows, :].astype(BF16)

            @pl.when(sub == 0)
            def _():
                for n, (side, at, _j) in enumerate(below):
                    target[side, base + at] = edge[taken + n, rows, :]

            @pl.when(sub == SUBS - 1)
            def _():
                for n, (side, at, _j) in enumerate(above):
                    target[side, base + at] = edge[taken + n, rows, :]

            base += tiles.shape[1]
            taken += len(below)


def split(tiles, edge):
    count = sum(t.shape[1] for t in tiles)
    shape = jax.ShapeDtypeStruct((2, count, WIDE, TILE), BF16)
    return pl.pallas_call(
        split_kernel,
        out_shape=[shape] * SUBS,
        in_specs=[VMEM] * 3,
        out_specs=[VMEM] * SUBS,
        compiler_params=pltpu.CompilerParams(vmem_limit_bytes=16 * MIB),
    )(*tiles, edge)


def gather_kernel(*refs):
    parts = refs[:4]
    out_ref, window = refs[4:]
    device, sub, parity = place()
    window[...] = jnp.zeros_like(window)
    for d in range(4):
        part = parts[d]
        first = 2 * (sub ^ d)
        at = 0
        for group in GROUPS:
            for chunk in group:
                for t in tiles_of(chunk):
                    for side in range(2):
                        column = 1 + chunk if side else -chunk
                        i = t if chunk < 2 else t + side
                        if 0 <= column - i + 4 < 7:
                            row = first + i - 1
                            row = jnp.where(row < 0, 7, jnp.where(row > 7, 0, row))
                            window[row, column - i + 4] += part[side, at].astype(F32)
                    at += 1
    out_ref[...] = window[...]


def gather_parts(parts):
    return pl.pallas_call(
        gather_kernel,
        out_shape=jax.ShapeDtypeStruct((8, 7, WIDE, TILE), F32),
        in_specs=[VMEM] * len(parts),
        out_specs=VMEM,
        scratch_shapes=[pltpu.VMEM((8, 7, WIDE, TILE), F32)],
        compiler_params=pltpu.CompilerParams(vmem_limit_bytes=16 * MIB),
    )(*parts)


def shards(a_tiles, a_cols, a_count, p_tiles, p_cols):
    fines = lax.axis_size("fine")
    total = fines * SUBS
    both = ("fine", "sub")
    pairs_a = [(i, i ^ 1) for i in range(total)]
    pairs_b = [(i, (i - 1 + 2 * (i % 2)) % total) for i in range(total)]
    hop = []
    for f in range(fines):
        for q in range(SUBS):
            other = f - 1 if q < SUBS // 2 else f + 1
            hop.append((f * SUBS + q, other % fines * SUBS + q))

    a0, b0 = collapse(p_tiles, p_cols)
    halo = [(lax.ppermute(a0, both, pairs_a), lax.ppermute(b0, both, pairs_b))]
    a1, b1, local, rh = first_half(a_tiles, a_cols, a_count, p_tiles, p_cols, a0, b0)
    halo.append((lax.ppermute(a1, both, pairs_a), lax.ppermute(b1, both, pairs_b)))
    local, rh = second_half(a_tiles, a_cols, a_count, a0, b0, a1, b1, local, rh)
    tiles, edges = [], []
    for group, (ha, hb) in zip(GROUPS, halo, strict=True):
        done, edge = finish(group, ha, hb, rh, local, *edges)
        tiles.append(done)
        edges = [edge]
    parts = list(split(tiles, lax.ppermute(edges[0], both, hop)))
    for d in range(1, SUBS):
        route = [(i, i ^ d) for i in range(SUBS)]
        parts[d] = lax.ppermute(parts[d], "sub", route)
    return gather_parts(parts)


def solution(mesh):
    in_specs = (
        P(("fine", "sub"), None, None, None),
        P(("fine", "sub"), None),
        P(("fine", "sub")),
        P(("fine", "sub"), None, None, None),
        P(("fine", "sub"), None),
    )
    out_specs = P("fine", None, "sub", None)
    return jax.shard_map(shards, mesh=mesh, in_specs=in_specs, out_specs=out_specs, check_vma=False)
```

```python
import jax
import jax.numpy as jnp
from jax import lax
from jax.experimental import pallas as pl
from jax.experimental.pallas import tpu as pltpu
from jax.sharding import PartitionSpec as P

AGG = 16
TILE = 128
SLOTS_A = 8
SLOTS_P = 4
ROWS = 32
SUBS = 4
WIDE = TILE // SUBS
F32 = jnp.float32
BF16 = jnp.bfloat16
MIB = 1 << 20
STEP = 4
GROUPS = ((0, 1), (2,))
PLAN = (((0,), (0, 1, 3)), ((1,), (0, 1, 3)), ((0, 1), (2,)))
VMEM = pl.BlockSpec(memory_space=pltpu.VMEM)
SMEM = pl.BlockSpec(memory_space=pltpu.SMEM)
HBM = pl.BlockSpec(memory_space=pltpu.HBM)


def place():
    fine = lax.axis_index("fine")
    sub = lax.axis_index("sub")
    return fine * SUBS + sub, sub, lax.rem(sub, 2)


def where_of(chunk):
    for g, group in enumerate(GROUPS):
        if chunk in group:
            return g, group.index(chunk)
    raise ValueError(chunk)


def fetch(source, target, sems, first, i):
    rows = pl.ds((first + i) * STEP, STEP)
    here = pl.ds(i * STEP, STEP)
    return pltpu.make_async_copy(source.at[rows], target.at[here], sems.at[i])


def collapse_rows(group, cols, p_hbm, held, sems, by_a, by_b, half):
    device, sub, parity = place()
    agg = device * 2 + half
    steps = AGG // STEP
    part = TILE // 4

    def fill(target):
        def rows_at(i, carry):
            first = half * steps + i
            fetch(p_hbm, held, sems, 0, first).wait()
            for r in range(STEP):
                row = first * STEP + r
                rel = [cols[k, row] - agg for k in range(SLOTS_P)]
                for q in range(4):
                    lines = slice(q * part, (q + 1) * part)
                    tiles = [held[row, k, lines].astype(F32) for k in range(SLOTS_P)]
                    for at, c in enumerate(group):
                        m = 1 - c if half == 1 else c - 1
                        value = jnp.where(rel[0] == m, tiles[0], 0.0)
                        for k in range(1, SLOTS_P):
                            value = value + jnp.where(rel[k] == m, tiles[k], 0.0)
                        target[at, i * STEP + r, lines] = value.astype(BF16)
            return carry

        lax.fori_loop(0, steps, rows_at, 0)

    @pl.when(parity == 1 - half)
    def _():
        fill(by_a)

    @pl.when(parity == half)
    def _():
        fill(by_b)


def collapse_kernel(cols, p_hbm, by_a, by_b, held, sems):
    for i in range(ROWS // STEP):
        fetch(p_hbm, held, sems, 0, i).start()
    for half in range(2):
        collapse_rows(GROUPS[0], cols, p_hbm, held, sems, by_a, by_b, half)


def collapse(p_tiles, p_cols):
    shape = jax.ShapeDtypeStruct((len(GROUPS[0]), AGG, TILE, TILE), BF16)
    return pl.pallas_call(
        collapse_kernel,
        out_shape=[shape, shape],
        in_specs=[SMEM, HBM],
        out_specs=[VMEM] * 2,
        scratch_shapes=[
            pltpu.VMEM((ROWS, SLOTS_P, TILE, TILE), BF16),
            pltpu.SemaphoreType.DMA((ROWS // STEP,)),
        ],
        compiler_params=pltpu.CompilerParams(vmem_limit_bytes=48 * MIB),
        cost_estimate=pl.CostEstimate(flops=8 * MIB, bytes_accessed=6 * MIB, transcendentals=0),
    )(p_cols.T, p_tiles)


def local_rows(half, acols, acount, a_hbm, by_a, by_b, out_ref, rh_ref, total, held, pc, sems):
    device, sub, parity = place()
    base = device * ROWS + half * AGG - AGG

    def spread(i, carry):
        for c in range(3):
            g, at = where_of(c)

            @pl.when(parity == 0)
            def _():
                pc[2 - c, AGG + i] = by_a[g][at, i]
                pc[c, i] = by_b[g][at, i]

            @pl.when(parity == 1)
            def _():
                pc[c, i] = by_a[g][at, i]
                pc[2 - c, AGG + i] = by_b[g][at, i]

        total[3 * i] = jnp.zeros((3 * TILE, TILE), F32)
        total[3 * i + 1] = jnp.zeros((3 * TILE, TILE), F32)
        total[3 * i + 2] = jnp.zeros((3 * TILE, TILE), F32)
        return carry

    lax.fori_loop(0, AGG, spread, 0)

    def rows_at(i, carry):
        fetch(a_hbm, held, sems, half * (AGG // STEP), i).wait()
        for r in range(STEP):
            near = i * STEP + r
            row = half * AGG + near
            own = jnp.concatenate([pc[m, row].T for m in range(3)], axis=0)
            used = acount[row]
            for k in range(0, SLOTS_A, 2):
                pair = jnp.concatenate([held[near, k], held[near, k + 1]], axis=1)
                both = jnp.dot(own, pair, preferred_element_type=F32)
                for e in range(2):
                    at = jnp.where(k + e < used, acols[k + e, row] - base, 3 * AGG)
                    total[at] += both[:, e * TILE : (e + 1) * TILE]
        return carry

    lax.fori_loop(0, AGG // STEP, rows_at, 0)
    for c in range(AGG):
        rh_ref[half, :, c * TILE : (c + 1) * TILE] = total[2 * AGG * half + c].astype(BF16)
    for o in range(5):
        out_ref[half, o] = jnp.zeros((3 * TILE, TILE), F32)
    for b in range(2):
        first = AGG * (b - half + 1)
        left = jnp.concatenate([total[first + c].astype(BF16) for c in range(AGG)], axis=1)
        right = jnp.concatenate(
            [pc[m, AGG * b : AGG * (b + 1)].reshape(AGG * TILE, TILE) for m in range(3)],
            axis=1,
        )
        part = jnp.dot(left, right, preferred_element_type=F32)
        for m in range(3):
            out_ref[half, b - half + 1 + m] += part[:, m * TILE : (m + 1) * TILE]


def first_kernel(
    acols, acount, cols, a_hbm, p_hbm, a0, b0, a1, b1, out_ref, rh_ref, total, held, pc, p_held, sems, p_sems
):
    for i in range(ROWS // STEP):
        fetch(p_hbm, p_held, p_sems, 0, i).start()
    for i in range(AGG // STEP):
        fetch(a_hbm, held, sems, 0, i).start()
    for half in range(2):
        collapse_rows(GROUPS[1], cols, p_hbm, p_held, p_sems, a1, b1, half)
    local_rows(
        0, acols, acount, a_hbm, (a0, a1), (b0, b1), out_ref, rh_ref, total, held, pc, sems
    )


def second_kernel(
    acols, acount, a_hbm, a0, b0, a1, b1, out_in, rh_in, out_ref, rh_ref, total, held, pc, sems
):
    for i in range(AGG // STEP):
        fetch(a_hbm, held, sems, AGG // STEP, i).start()
    local_rows(
        1, acols, acount, a_hbm, (a0, a1), (b0, b1), out_ref, rh_ref, total, held, pc, sems
    )


LOCAL = [
    jax.ShapeDtypeStruct((2, 5, 3 * TILE, TILE), F32),
    jax.ShapeDtypeStruct((2, 3 * TILE, AGG * TILE), BF16),
]


def scratch():
    return [
        pltpu.VMEM((3 * AGG + 1, 3 * TILE, TILE), F32),
        pltpu.VMEM((AGG, SLOTS_A, TILE, TILE), BF16),
        pltpu.VMEM((3, ROWS, TILE, TILE), BF16),
    ]


def first_half(a_tiles, a_cols, a_count, p_tiles, p_cols, a0, b0):
    shape = jax.ShapeDtypeStruct((len(GROUPS[1]), AGG, TILE, TILE), BF16)
    return pl.pallas_call(
        first_kernel,
        out_shape=[shape, shape] + LOCAL,
        in_specs=[SMEM, SMEM, SMEM, HBM, HBM, VMEM, VMEM],
        out_specs=[VMEM] * 4,
        scratch_shapes=scratch()
        + [
            pltpu.VMEM((ROWS, SLOTS_P, TILE, TILE), BF16),
            pltpu.SemaphoreType.DMA((AGG // STEP,)),
            pltpu.SemaphoreType.DMA((ROWS // STEP,)),
        ],
        compiler_params=pltpu.CompilerParams(vmem_limit_bytes=40 * MIB),
        cost_estimate=pl.CostEstimate(
            flops=8 * 1024 * MIB, bytes_accessed=8 * MIB, transcendentals=0
        ),
    )(a_cols.T, a_count, p_cols.T, a_tiles, p_tiles, a0, b0)


def second_half(a_tiles, a_cols, a_count, a0, b0, a1, b1, local, rh):
    return pl.pallas_call(
        second_kernel,
        out_shape=LOCAL,
        in_specs=[SMEM, SMEM, HBM] + [VMEM] * 6,
        out_specs=[VMEM] * 2,
        scratch_shapes=scratch() + [pltpu.SemaphoreType.DMA((AGG // STEP,))],
        input_output_aliases={7: 0, 8: 1},
        compiler_params=pltpu.CompilerParams(vmem_limit_bytes=40 * MIB),
        cost_estimate=pl.CostEstimate(
            flops=8 * 1024 * MIB, bytes_accessed=8 * MIB, transcendentals=0
        ),
    )(a_cols.T, a_count, a_tiles, a0, b0, a1, b1, local, rh)


def tiles_of(chunk):
    return (0, 1, 2, 3) if chunk < 2 else (0, 1, 2)


def edge_tiles(group):
    below, above, at = [], [], 0
    for chunk in group:
        for t in tiles_of(chunk):
            for side in range(2):
                i = t if chunk < 2 else t + side
                column = 1 + chunk if side else -chunk
                if i == 0:
                    below.append((side, at, column + 4))
                if i == 3:
                    above.append((side, at, column + 1))
            at += 1
    below = [b for b in below if 2 <= b[2] < 7]
    above = [b for b in above if 0 <= b[2] < 5]
    return sorted(below, key=lambda b: b[2]), sorted(above, key=lambda b: b[2])


def finish_kernel(group, ha_ref, hb_ref, rh_ref, out_ref, tiles, edge):
    device, sub, parity = place()
    for x, halo in enumerate((ha_ref, hb_ref)):
        side = x ^ (1 - parity)
        right = jnp.concatenate(
            [halo[at].reshape(AGG * TILE, TILE) for at in range(len(group))], axis=1
        )
        parts = jnp.dot(rh_ref[side], right, preferred_element_type=F32)
        first = 0
        for at, chunk in enumerate(group):
            part = parts[:, at * TILE : (at + 1) * TILE]
            part = part + out_ref[side, jnp.where(side == 0, 2 - chunk, 2 + chunk)]
            if chunk < 2:
                other = out_ref[1 - side, jnp.where(side == 0, 1 - chunk, 3 + chunk)]
                low = jnp.where(side == 0, part, other)
                high = jnp.where(side == 0, other, part)
                tiles[side, first] = low[:TILE]
                tiles[side, first + 1] = low[TILE : 2 * TILE] + high[:TILE]
                tiles[side, first + 2] = low[2 * TILE :] + high[TILE : 2 * TILE]
                tiles[side, first + 3] = high[2 * TILE :]
            else:
                for t in range(3):
                    tiles[side, first + t] = part[t * TILE : (t + 1) * TILE]
            first += len(tiles_of(chunk))
    below, above = edge_tiles(group)

    @pl.when(sub == 0)
    def _():
        for n, (side, at, _j) in enumerate(below):
            edge[n] = tiles[side, at].astype(BF16)

    @pl.when(sub == SUBS - 1)
    def _():
        for n, (side, at, _j) in enumerate(above):
            edge[n] = tiles[side, at].astype(BF16)


def finish(group, ha, hb, rh, local):
    count = sum(len(tiles_of(c)) for c in group)
    edges = len(edge_tiles(group)[0])

    def kernel(*refs):
        finish_kernel(group, *refs)

    return pl.pallas_call(
        kernel,
        out_shape=[
            jax.ShapeDtypeStruct((2, count, TILE, TILE), F32),
            jax.ShapeDtypeStruct((edges, TILE, TILE), BF16),
        ],
        in_specs=[VMEM] * 4,
        out_specs=[VMEM] * 2,
        compiler_params=pltpu.CompilerParams(vmem_limit_bytes=24 * MIB),
        cost_estimate=pl.CostEstimate(
            flops=400 * MIB, bytes_accessed=6 * MIB, transcendentals=0
        ),
    )(ha, hb, rh, local)


def split_kernel(groups, which, *refs):
    device, sub, parity = place()
    last = device >= (lax.axis_size("fine") - 1) * SUBS
    for d, target in zip(which, refs[2 * len(groups) :], strict=True):
        rows = pl.ds(pl.multiple_of((sub ^ d) * WIDE, WIDE), WIDE)
        base = 0
        for n_group, g in enumerate(groups):
            tiles, edge = refs[2 * n_group : 2 * n_group + 2]
            below, above = edge_tiles(GROUPS[g])
            for side in range(2):
                for i in range(tiles.shape[1]):
                    target[side, base + i] = tiles[side, i, rows, :].astype(BF16)

            @pl.when(sub == 0)
            def _():
                for n, (side, at, _j) in enumerate(below):
                    kept = jnp.where(last, 0.0, edge[n, rows, :].astype(F32))
                    target[side, base + at] = kept.astype(BF16)

            @pl.when(sub == SUBS - 1)
            def _():
                for n, (side, at, _j) in enumerate(above):
                    kept = jnp.where(device < SUBS, 0.0, edge[n, rows, :].astype(F32))
                    target[side, base + at] = kept.astype(BF16)

            base += tiles.shape[1]


def split(groups, which, tiles, edges):
    count = sum(tiles[g].shape[1] for g in groups)
    shape = jax.ShapeDtypeStruct((2, count, WIDE, TILE), BF16)

    def kernel(*refs):
        split_kernel(groups, which, *refs)

    return pl.pallas_call(
        kernel,
        out_shape=[shape] * len(which),
        in_specs=[VMEM] * (2 * len(groups)),
        out_specs=[VMEM] * len(which),
        compiler_params=pltpu.CompilerParams(vmem_limit_bytes=16 * MIB),
    )(*[x for g in groups for x in (tiles[g], edges[g])])


def gather_kernel(kinds, *refs):
    parts = refs[: len(kinds)]
    out_ref, window = refs[len(kinds) :]
    device, sub, parity = place()
    window[...] = jnp.zeros_like(window)
    for (d, groups), part in zip(kinds, parts, strict=True):
        first = 2 * (sub ^ d)
        at = 0
        for chunk in [c for g in groups for c in GROUPS[g]]:
            for t in tiles_of(chunk):
                for side in range(2):
                    column = 1 + chunk if side else -chunk
                    i = t if chunk < 2 else t + side
                    if 0 <= column - i + 4 < 7:
                        row = first + i - 1
                        row = jnp.where(row < 0, 7, jnp.where(row > 7, 0, row))
                        window[row, column - i + 4] += part[side, at].astype(F32)
                at += 1
    out_ref[...] = window[...]


def gather_parts(kinds, parts):
    def kernel(*refs):
        gather_kernel(kinds, *refs)

    return pl.pallas_call(
        kernel,
        out_shape=jax.ShapeDtypeStruct((8, 7, WIDE, TILE), F32),
        in_specs=[VMEM] * len(parts),
        out_specs=VMEM,
        scratch_shapes=[pltpu.VMEM((8, 7, WIDE, TILE), F32)],
        compiler_params=pltpu.CompilerParams(vmem_limit_bytes=16 * MIB),
    )(*parts)


def shards(a_tiles, a_cols, a_count, p_tiles, p_cols):
    fines = lax.axis_size("fine")
    total = fines * SUBS
    both = ("fine", "sub")
    pairs_a = [(i, i ^ 1) for i in range(total)]
    pairs_b = [(i, (i - 1 + 2 * (i % 2)) % total) for i in range(total)]
    hop = []
    for q, other, step in ((0, 1, -1), (3, 2, 1)):
        down = [f * SUBS + q for f in range(fines)][::step]
        back = [f * SUBS + other for f in range(fines)][::-step]
        loop = down + back
        hop += list(zip(loop, loop[1:] + loop[:1], strict=True))

    a0, b0 = collapse(p_tiles, p_cols)
    halo = [(lax.ppermute(a0, both, pairs_a), lax.ppermute(b0, both, pairs_b))]
    a1, b1, local, rh = first_half(a_tiles, a_cols, a_count, p_tiles, p_cols, a0, b0)
    halo.append((lax.ppermute(a1, both, pairs_a), lax.ppermute(b1, both, pairs_b)))
    local, rh = second_half(a_tiles, a_cols, a_count, a0, b0, a1, b1, local, rh)
    done = [finish(group, ha, hb, rh, local) for group, (ha, hb) in zip(GROUPS, halo, strict=True)]
    tiles = [t for t, _ in done]
    edges = [lax.ppermute(edge, both, hop) for _, edge in done]
    kinds, parts = [], []
    for groups, which in PLAN:
        for d, part in zip(which, split(groups, which, tiles, edges), strict=True):
            if d:
                part = lax.ppermute(part, "sub", [(i, i ^ d) for i in range(SUBS)])
            kinds.append((d, groups))
            parts.append(part)
    return gather_parts(kinds, parts)


def solution(mesh):
    in_specs = (
        P(("fine", "sub"), None, None, None),
        P(("fine", "sub"), None),
        P(("fine", "sub")),
        P(("fine", "sub"), None, None, None),
        P(("fine", "sub"), None),
    )
    out_specs = P("fine", None, "sub", None)
    return jax.shard_map(shards, mesh=mesh, in_specs=in_specs, out_specs=out_specs, check_vma=False)
```

```python
import jax
import jax.numpy as jnp
from jax import lax
from jax.experimental import pallas as pl
from jax.experimental.pallas import tpu as pltpu
from jax.sharding import PartitionSpec as P

AGG = 16
TILE = 128
SLOTS_A = 8
SLOTS_P = 4
ROWS = 32
SUBS = 4
WIDE = TILE // SUBS
F32 = jnp.float32
BF16 = jnp.bfloat16
MIB = 1 << 20
STEP = 4
GROUPS = ((0, 1), (2,))
PLAN = (((0, 1), (2,)), ((0, 1), (0, 1, 3)))
VMEM = pl.BlockSpec(memory_space=pltpu.VMEM)
SMEM = pl.BlockSpec(memory_space=pltpu.SMEM)
HBM = pl.BlockSpec(memory_space=pltpu.HBM)


def place():
    fine = lax.axis_index("fine")
    sub = lax.axis_index("sub")
    return fine * SUBS + sub, sub, lax.rem(sub, 2)


def where_of(chunk):
    for g, group in enumerate(GROUPS):
        if chunk in group:
            return g, group.index(chunk)
    raise ValueError(chunk)


def fetch(source, target, sems, first, i):
    rows = pl.ds((first + i) * STEP, STEP)
    here = pl.ds(i * STEP, STEP)
    return pltpu.make_async_copy(source.at[rows], target.at[here], sems.at[i])


def collapse_rows(group, cols, p_hbm, held, sems, by_a, by_b, half):
    device, sub, parity = place()
    agg = device * 2 + half
    steps = AGG // STEP
    part = TILE // 4

    def fill(target):
        def rows_at(i, carry):
            first = half * steps + i
            fetch(p_hbm, held, sems, 0, first).wait()
            for r in range(STEP):
                row = first * STEP + r
                rel = [cols[k, row] - agg for k in range(SLOTS_P)]
                for q in range(4):
                    lines = slice(q * part, (q + 1) * part)
                    tiles = [held[row, k, lines].astype(F32) for k in range(SLOTS_P)]
                    for at, c in enumerate(group):
                        m = 1 - c if half == 1 else c - 1
                        value = jnp.where(rel[0] == m, tiles[0], 0.0)
                        for k in range(1, SLOTS_P):
                            value = value + jnp.where(rel[k] == m, tiles[k], 0.0)
                        target[at, i * STEP + r, lines] = value.astype(BF16)
            return carry

        lax.fori_loop(0, steps, rows_at, 0)

    @pl.when(parity == 1 - half)
    def _():
        fill(by_a)

    @pl.when(parity == half)
    def _():
        fill(by_b)


def collapse_kernel(cols, p_hbm, by_a, by_b, held, sems):
    for i in range(ROWS // STEP):
        fetch(p_hbm, held, sems, 0, i).start()
    for half in range(2):
        collapse_rows(GROUPS[0], cols, p_hbm, held, sems, by_a, by_b, half)


def collapse(p_tiles, p_cols):
    shape = jax.ShapeDtypeStruct((len(GROUPS[0]), AGG, TILE, TILE), BF16)
    return pl.pallas_call(
        collapse_kernel,
        out_shape=[shape, shape],
        in_specs=[SMEM, HBM],
        out_specs=[VMEM] * 2,
        scratch_shapes=[
            pltpu.VMEM((ROWS, SLOTS_P, TILE, TILE), BF16),
            pltpu.SemaphoreType.DMA((ROWS // STEP,)),
        ],
        compiler_params=pltpu.CompilerParams(vmem_limit_bytes=48 * MIB),
        cost_estimate=pl.CostEstimate(flops=8 * MIB, bytes_accessed=6 * MIB, transcendentals=0),
    )(p_cols.T, p_tiles)


def local_rows(half, acols, acount, a_hbm, by_a, by_b, out_ref, rh_ref, total, held, pc, sems):
    device, sub, parity = place()
    base = device * ROWS + half * AGG - AGG

    def spread(i, carry):
        for c in range(3):
            g, at = where_of(c)

            @pl.when(parity == 0)
            def _():
                pc[2 - c, AGG + i] = by_a[g][at, i]
                pc[c, i] = by_b[g][at, i]

            @pl.when(parity == 1)
            def _():
                pc[c, i] = by_a[g][at, i]
                pc[2 - c, AGG + i] = by_b[g][at, i]

        total[3 * i] = jnp.zeros((3 * TILE, TILE), F32)
        total[3 * i + 1] = jnp.zeros((3 * TILE, TILE), F32)
        total[3 * i + 2] = jnp.zeros((3 * TILE, TILE), F32)
        return carry

    lax.fori_loop(0, AGG, spread, 0)

    def rows_at(i, carry):
        fetch(a_hbm, held, sems, half * (AGG // STEP), i).wait()
        for r in range(STEP):
            near = i * STEP + r
            row = half * AGG + near
            own = jnp.concatenate([pc[m, row].T for m in range(3)], axis=0)
            used = acount[row]
            for k in range(0, SLOTS_A, 2):
                pair = jnp.concatenate([held[near, k], held[near, k + 1]], axis=1)
                both = jnp.dot(own, pair, preferred_element_type=F32)
                for e in range(2):
                    at = jnp.where(k + e < used, acols[k + e, row] - base, 3 * AGG)
                    total[at] += both[:, e * TILE : (e + 1) * TILE]
        return carry

    lax.fori_loop(0, AGG // STEP, rows_at, 0)
    for c in range(AGG):
        rh_ref[half, :, c * TILE : (c + 1) * TILE] = total[2 * AGG * half + c].astype(BF16)
    for o in range(5):
        out_ref[half, o] = jnp.zeros((3 * TILE, TILE), F32)
    for b in range(2):
        first = AGG * (b - half + 1)
        left = jnp.concatenate([total[first + c].astype(BF16) for c in range(AGG)], axis=1)
        right = jnp.concatenate(
            [pc[m, AGG * b : AGG * (b + 1)].reshape(AGG * TILE, TILE) for m in range(3)],
            axis=1,
        )
        part = jnp.dot(left, right, preferred_element_type=F32)
        for m in range(3):
            out_ref[half, b - half + 1 + m] += part[:, m * TILE : (m + 1) * TILE]


def first_kernel(
    acols, acount, cols, a_hbm, p_hbm, a0, b0, a1, b1, out_ref, rh_ref, total, held, pc, p_held, sems, p_sems
):
    for i in range(ROWS // STEP):
        fetch(p_hbm, p_held, p_sems, 0, i).start()
    for i in range(AGG // STEP):
        fetch(a_hbm, held, sems, 0, i).start()
    for half in range(2):
        collapse_rows(GROUPS[1], cols, p_hbm, p_held, p_sems, a1, b1, half)
    local_rows(
        0, acols, acount, a_hbm, (a0, a1), (b0, b1), out_ref, rh_ref, total, held, pc, sems
    )


def second_kernel(
    acols, acount, a_hbm, a0, b0, a1, b1, out_in, rh_in, out_ref, rh_ref, total, held, pc, sems
):
    for i in range(AGG // STEP):
        fetch(a_hbm, held, sems, AGG // STEP, i).start()
    local_rows(
        1, acols, acount, a_hbm, (a0, a1), (b0, b1), out_ref, rh_ref, total, held, pc, sems
    )


LOCAL = [
    jax.ShapeDtypeStruct((2, 5, 3 * TILE, TILE), F32),
    jax.ShapeDtypeStruct((2, 3 * TILE, AGG * TILE), BF16),
]


def scratch():
    return [
        pltpu.VMEM((3 * AGG + 1, 3 * TILE, TILE), F32),
        pltpu.VMEM((AGG, SLOTS_A, TILE, TILE), BF16),
        pltpu.VMEM((3, ROWS, TILE, TILE), BF16),
    ]


def first_half(a_tiles, a_cols, a_count, p_tiles, p_cols, a0, b0):
    shape = jax.ShapeDtypeStruct((len(GROUPS[1]), AGG, TILE, TILE), BF16)
    return pl.pallas_call(
        first_kernel,
        out_shape=[shape, shape] + LOCAL,
        in_specs=[SMEM, SMEM, SMEM, HBM, HBM, VMEM, VMEM],
        out_specs=[VMEM] * 4,
        scratch_shapes=scratch()
        + [
            pltpu.VMEM((ROWS, SLOTS_P, TILE, TILE), BF16),
            pltpu.SemaphoreType.DMA((AGG // STEP,)),
            pltpu.SemaphoreType.DMA((ROWS // STEP,)),
        ],
        compiler_params=pltpu.CompilerParams(vmem_limit_bytes=40 * MIB),
        cost_estimate=pl.CostEstimate(
            flops=8 * 1024 * MIB, bytes_accessed=8 * MIB, transcendentals=0
        ),
    )(a_cols.T, a_count, p_cols.T, a_tiles, p_tiles, a0, b0)


def second_half(a_tiles, a_cols, a_count, a0, b0, a1, b1, local, rh):
    return pl.pallas_call(
        second_kernel,
        out_shape=LOCAL,
        in_specs=[SMEM, SMEM, HBM] + [VMEM] * 6,
        out_specs=[VMEM] * 2,
        scratch_shapes=scratch() + [pltpu.SemaphoreType.DMA((AGG // STEP,))],
        input_output_aliases={7: 0, 8: 1},
        compiler_params=pltpu.CompilerParams(vmem_limit_bytes=40 * MIB),
        cost_estimate=pl.CostEstimate(
            flops=8 * 1024 * MIB, bytes_accessed=8 * MIB, transcendentals=0
        ),
    )(a_cols.T, a_count, a_tiles, a0, b0, a1, b1, local, rh)


def tiles_of(chunk):
    return (0, 1, 2, 3) if chunk < 2 else (0, 1, 2)


def edge_tiles(group):
    below, above, at = [], [], 0
    for chunk in group:
        for t in tiles_of(chunk):
            for side in range(2):
                i = t if chunk < 2 else t + side
                column = 1 + chunk if side else -chunk
                if i == 0:
                    below.append((side, at, column + 4))
                if i == 3:
                    above.append((side, at, column + 1))
            at += 1
    below = [b for b in below if 2 <= b[2] < 7]
    above = [b for b in above if 0 <= b[2] < 5]
    return sorted(below, key=lambda b: b[2]), sorted(above, key=lambda b: b[2])


def finish_kernel(group, ha_ref, hb_ref, rh_ref, out_ref, tiles, *edge):
    device, sub, parity = place()
    for x, halo in enumerate((ha_ref, hb_ref)):
        side = x ^ (1 - parity)
        right = jnp.concatenate(
            [halo[at].reshape(AGG * TILE, TILE) for at in range(len(group))], axis=1
        )
        parts = jnp.dot(rh_ref[side], right, preferred_element_type=F32)
        first = 0
        for at, chunk in enumerate(group):
            part = parts[:, at * TILE : (at + 1) * TILE]
            part = part + out_ref[side, jnp.where(side == 0, 2 - chunk, 2 + chunk)]
            if chunk < 2:
                other = out_ref[1 - side, jnp.where(side == 0, 1 - chunk, 3 + chunk)]
                low = jnp.where(side == 0, part, other)
                high = jnp.where(side == 0, other, part)
                tiles[side, first] = low[:TILE]
                tiles[side, first + 1] = low[TILE : 2 * TILE] + high[:TILE]
                tiles[side, first + 2] = low[2 * TILE :] + high[TILE : 2 * TILE]
                tiles[side, first + 3] = high[2 * TILE :]
            else:
                for t in range(3):
                    tiles[side, first + t] = part[t * TILE : (t + 1) * TILE]
            first += len(tiles_of(chunk))
    if not edge:
        return
    below, above = edge_tiles(group)

    @pl.when(sub == 0)
    def _():
        for n, (side, at, _j) in enumerate(below):
            edge[0][n] = tiles[side, at].astype(BF16)

    @pl.when(sub == SUBS - 1)
    def _():
        for n, (side, at, _j) in enumerate(above):
            edge[0][n] = tiles[side, at].astype(BF16)


def last_edge_kernel(hb_ref, rh_ref, out_ref, edge):
    device, sub, parity = place()

    def one(side, t):
        rows = slice(t * TILE, (t + 1) * TILE)
        part = jnp.dot(
            rh_ref[side, rows, :], hb_ref[0].reshape(AGG * TILE, TILE), preferred_element_type=F32
        )
        edge[0] = (part + out_ref[side, 4 * side, rows]).astype(BF16)

    @pl.when(sub < SUBS - 1)
    def _():
        one(0, 0)

    @pl.when(sub == SUBS - 1)
    def _():
        one(1, 2)


def last_edge(hb, rh, local):
    return pl.pallas_call(
        last_edge_kernel,
        out_shape=jax.ShapeDtypeStruct((1, TILE, TILE), BF16),
        in_specs=[VMEM] * 3,
        out_specs=VMEM,
        compiler_params=pltpu.CompilerParams(vmem_limit_bytes=24 * MIB),
        cost_estimate=pl.CostEstimate(flops=64 * MIB, bytes_accessed=MIB, transcendentals=0),
    )(hb, rh, local)


def finish(group, with_edge, ha, hb, rh, local, *after):
    count = sum(len(tiles_of(c)) for c in group)
    shapes = [jax.ShapeDtypeStruct((2, count, TILE, TILE), F32)]
    if with_edge:
        edges = len(edge_tiles(group)[0])
        shapes.append(jax.ShapeDtypeStruct((edges, TILE, TILE), BF16))

    def kernel(*refs):
        finish_kernel(group, *refs[:4], *refs[4 + len(after) :])

    return pl.pallas_call(
        kernel,
        out_shape=shapes,
        in_specs=[VMEM] * (4 + len(after)),
        out_specs=[VMEM] * len(shapes),
        compiler_params=pltpu.CompilerParams(vmem_limit_bytes=24 * MIB),
        cost_estimate=pl.CostEstimate(
            flops=400 * MIB, bytes_accessed=6 * MIB, transcendentals=0
        ),
    )(ha, hb, rh, local, *after)


def split_kernel(groups, which, *refs):
    device, sub, parity = place()
    last = device >= (lax.axis_size("fine") - 1) * SUBS
    for d, target in zip(which, refs[2 * len(groups) :], strict=True):
        rows = pl.ds(pl.multiple_of((sub ^ d) * WIDE, WIDE), WIDE)
        base = 0
        for n_group, g in enumerate(groups):
            tiles, edge = refs[2 * n_group : 2 * n_group + 2]
            below, above = edge_tiles(GROUPS[g])
            for side in range(2):
                for i in range(tiles.shape[1]):
                    target[side, base + i] = tiles[side, i, rows, :].astype(BF16)

            @pl.when(sub == 0)
            def _():
                for n, (side, at, _j) in enumerate(below):
                    kept = jnp.where(last, 0.0, edge[n, rows, :].astype(F32))
                    target[side, base + at] = kept.astype(BF16)

            @pl.when(sub == SUBS - 1)
            def _():
                for n, (side, at, _j) in enumerate(above):
                    kept = jnp.where(device < SUBS, 0.0, edge[n, rows, :].astype(F32))
                    target[side, base + at] = kept.astype(BF16)

            base += tiles.shape[1]


def split(groups, which, tiles, edges, *after):
    count = sum(tiles[g].shape[1] for g in groups)
    shape = jax.ShapeDtypeStruct((2, count, WIDE, TILE), BF16)

    def kernel(*refs):
        split_kernel(groups, which, *refs[: 2 * len(groups)], *refs[2 * len(groups) + len(after) :])

    return pl.pallas_call(
        kernel,
        out_shape=[shape] * len(which),
        in_specs=[VMEM] * (2 * len(groups) + len(after)),
        out_specs=[VMEM] * len(which),
        compiler_params=pltpu.CompilerParams(vmem_limit_bytes=16 * MIB),
    )(*[x for g in groups for x in (tiles[g], edges[g])], *after)


def gather_kernel(kinds, *refs):
    parts = refs[: len(kinds)]
    out_ref = refs[len(kinds)]
    device, sub, parity = place()
    out_ref[...] = jnp.zeros_like(out_ref)
    for (d, groups), part in zip(kinds, parts, strict=True):
        first = 2 * (sub ^ d)
        at = 0
        for chunk in [c for g in groups for c in GROUPS[g]]:
            for t in tiles_of(chunk):
                for side in range(2):
                    column = 1 + chunk if side else -chunk
                    i = t if chunk < 2 else t + side
                    if 0 <= column - i + 4 < 7:
                        row = first + i - 1
                        row = jnp.where(row < 0, 7, jnp.where(row > 7, 0, row))
                        out_ref[row, column - i + 4] += part[side, at].astype(F32)
                at += 1


def gather_parts(kinds, parts):
    def kernel(*refs):
        gather_kernel(kinds, *refs)

    return pl.pallas_call(
        kernel,
        out_shape=jax.ShapeDtypeStruct((8, 7, WIDE, TILE), F32),
        in_specs=[VMEM] * len(parts),
        out_specs=VMEM,
        compiler_params=pltpu.CompilerParams(vmem_limit_bytes=16 * MIB),
    )(*parts)


def shards(a_tiles, a_cols, a_count, p_tiles, p_cols):
    fines = lax.axis_size("fine")
    total = fines * SUBS
    both = ("fine", "sub")
    pairs_a = [(i, i ^ 1) for i in range(total)]
    pairs_b = [(i, (i - 1 + 2 * (i % 2)) % total) for i in range(total)]
    hop = []
    for q, other, step in ((0, 1, -1), (3, 2, 1)):
        down = [f * SUBS + q for f in range(fines)][::step]
        back = [f * SUBS + other for f in range(fines)][::-step]
        loop = down + back
        hop += list(zip(loop, loop[1:] + loop[:1], strict=True))

    a0, b0 = collapse(p_tiles, p_cols)
    halo = [(lax.ppermute(a0, both, pairs_a), lax.ppermute(b0, both, pairs_b))]
    a1, b1, local, rh = first_half(a_tiles, a_cols, a_count, p_tiles, p_cols, a0, b0)
    halo.append((lax.ppermute(a1, both, pairs_a), lax.ppermute(b1, both, pairs_b)))
    local, rh = second_half(a_tiles, a_cols, a_count, a0, b0, a1, b1, local, rh)
    tiles0, edge0 = finish(GROUPS[0], True, *halo[0], rh, local)
    edge1 = last_edge(halo[1][1], rh, local)
    (tiles1,) = finish(GROUPS[1], False, *halo[1], rh, local, edge1)
    tiles = [tiles0, tiles1]
    edges = [lax.ppermute(edge, both, hop) for edge in (edge0, edge1)]
    kinds, parts, first = [], [], []
    for groups, which in PLAN:
        cut = split(groups, which, tiles, edges, *first)
        first = cut if len(which) == 1 else []
        for d, part in zip(which, cut, strict=True):
            if d:
                part = lax.ppermute(part, "sub", [(i, i ^ d) for i in range(SUBS)])
            kinds.append((d, groups))
            parts.append(part)
    return gather_parts(kinds, parts)


def solution(mesh):
    in_specs = (
        P(("fine", "sub"), None, None, None),
        P(("fine", "sub"), None),
        P(("fine", "sub")),
        P(("fine", "sub"), None, None, None),
        P(("fine", "sub"), None),
    )
    out_specs = P("fine", None, "sub", None)
    return jax.shard_map(shards, mesh=mesh, in_specs=in_specs, out_specs=out_specs, check_vma=False)
```

```python
import jax
import jax.numpy as jnp
from jax import lax
from jax.experimental import pallas as pl
from jax.experimental.pallas import tpu as pltpu
from jax.sharding import PartitionSpec as P

AGG = 16
TILE = 128
SLOTS_A = 8
SLOTS_P = 4
ROWS = 32
SUBS = 4
WIDE = TILE // SUBS
F32 = jnp.float32
BF16 = jnp.bfloat16
MIB = 1 << 20
STEP = 4
GROUPS = ((0, 1), (2,))
PLAN = (((0, 1), (2,)), ((0, 1), (0, 1, 3)))
VMEM = pl.BlockSpec(memory_space=pltpu.VMEM)
SMEM = pl.BlockSpec(memory_space=pltpu.SMEM)
HBM = pl.BlockSpec(memory_space=pltpu.HBM)


def place():
    fine = lax.axis_index("fine")
    sub = lax.axis_index("sub")
    return fine * SUBS + sub, sub, lax.rem(sub, 2)


def where_of(chunk):
    for g, group in enumerate(GROUPS):
        if chunk in group:
            return g, group.index(chunk)
    raise ValueError(chunk)


def fetch(source, target, sems, first, i):
    rows = pl.ds((first + i) * STEP, STEP)
    here = pl.ds(i * STEP, STEP)
    return pltpu.make_async_copy(source.at[rows], target.at[here], sems.at[i])


def collapse_rows(group, cols, p_hbm, held, sems, by_a, by_b, half):
    device, sub, parity = place()
    agg = device * 2 + half
    steps = AGG // STEP
    part = TILE // 4

    def fill(target):
        def rows_at(i, carry):
            first = half * steps + i
            fetch(p_hbm, held, sems, 0, first).wait()
            for r in range(STEP):
                row = first * STEP + r
                rel = [cols[k, row] - agg for k in range(SLOTS_P)]
                for q in range(4):
                    lines = slice(q * part, (q + 1) * part)
                    tiles = [held[row, k, lines].astype(F32) for k in range(SLOTS_P)]
                    for at, c in enumerate(group):
                        m = 1 - c if half == 1 else c - 1
                        value = jnp.where(rel[0] == m, tiles[0], 0.0)
                        for k in range(1, SLOTS_P):
                            value = value + jnp.where(rel[k] == m, tiles[k], 0.0)
                        target[at, i * STEP + r, lines] = value.astype(BF16)
            return carry

        lax.fori_loop(0, steps, rows_at, 0)

    @pl.when(parity == 1 - half)
    def _():
        fill(by_a)

    @pl.when(parity == half)
    def _():
        fill(by_b)


def collapse_kernel(cols, p_hbm, by_a, by_b, held, sems):
    for i in range(ROWS // STEP):
        fetch(p_hbm, held, sems, 0, i).start()
    for half in range(2):
        collapse_rows(GROUPS[0], cols, p_hbm, held, sems, by_a, by_b, half)


def collapse(p_tiles, p_cols):
    shape = jax.ShapeDtypeStruct((len(GROUPS[0]), AGG, TILE, TILE), BF16)
    return pl.pallas_call(
        collapse_kernel,
        out_shape=[shape, shape],
        in_specs=[SMEM, HBM],
        out_specs=[VMEM] * 2,
        scratch_shapes=[
            pltpu.VMEM((ROWS, SLOTS_P, TILE, TILE), BF16),
            pltpu.SemaphoreType.DMA((ROWS // STEP,)),
        ],
        compiler_params=pltpu.CompilerParams(vmem_limit_bytes=48 * MIB),
        cost_estimate=pl.CostEstimate(flops=8 * MIB, bytes_accessed=6 * MIB, transcendentals=0),
    )(p_cols.T, p_tiles)


def local_rows(half, acols, acount, a_hbm, by_a, by_b, out_ref, rh_ref, total, held, pc, sems):
    device, sub, parity = place()
    base = device * ROWS + half * AGG - AGG

    def spread(i, carry):
        for c in range(3):
            g, at = where_of(c)

            @pl.when(parity == 0)
            def _():
                pc[2 - c, AGG + i] = by_a[g][at, i]
                pc[c, i] = by_b[g][at, i]

            @pl.when(parity == 1)
            def _():
                pc[c, i] = by_a[g][at, i]
                pc[2 - c, AGG + i] = by_b[g][at, i]

        total[3 * i] = jnp.zeros((3 * TILE, TILE), F32)
        total[3 * i + 1] = jnp.zeros((3 * TILE, TILE), F32)
        total[3 * i + 2] = jnp.zeros((3 * TILE, TILE), F32)
        return carry

    lax.fori_loop(0, AGG, spread, 0)

    def rows_at(i, carry):
        fetch(a_hbm, held, sems, half * (AGG // STEP), i).wait()
        for r in range(STEP):
            near = i * STEP + r
            row = half * AGG + near
            own = jnp.concatenate([pc[m, row].T for m in range(3)], axis=0)
            used = acount[row]
            for k in range(0, SLOTS_A, 2):
                pair = jnp.concatenate([held[near, k], held[near, k + 1]], axis=1)
                both = jnp.dot(own, pair, preferred_element_type=F32)
                for e in range(2):
                    at = jnp.where(k + e < used, acols[k + e, row] - base, 3 * AGG)
                    total[at] += both[:, e * TILE : (e + 1) * TILE]
        return carry

    lax.fori_loop(0, AGG // STEP, rows_at, 0)
    for c in range(AGG):
        rh_ref[half, :, c * TILE : (c + 1) * TILE] = total[2 * AGG * half + c].astype(BF16)
    for o in range(5):
        out_ref[half, o] = jnp.zeros((3 * TILE, TILE), F32)
    for b in range(2):
        first = AGG * (b - half + 1)
        left = jnp.concatenate([total[first + c].astype(BF16) for c in range(AGG)], axis=1)
        right = jnp.concatenate(
            [pc[m, AGG * b : AGG * (b + 1)].reshape(AGG * TILE, TILE) for m in range(3)],
            axis=1,
        )
        part = jnp.dot(left, right, preferred_element_type=F32)
        for m in range(3):
            out_ref[half, b - half + 1 + m] += part[:, m * TILE : (m + 1) * TILE]


def first_kernel(
    acols, acount, cols, a_hbm, p_hbm, a0, b0, a1, b1, out_ref, rh_ref, total, held, pc, p_held, sems, p_sems
):
    for i in range(ROWS // STEP):
        fetch(p_hbm, p_held, p_sems, 0, i).start()
    for i in range(AGG // STEP):
        fetch(a_hbm, held, sems, 0, i).start()
    for half in range(2):
        collapse_rows(GROUPS[1], cols, p_hbm, p_held, p_sems, a1, b1, half)
    local_rows(
        0, acols, acount, a_hbm, (a0, a1), (b0, b1), out_ref, rh_ref, total, held, pc, sems
    )


def second_kernel(
    acols, acount, a_hbm, a0, b0, a1, b1, out_in, rh_in, out_ref, rh_ref, total, held, pc, sems
):
    for i in range(AGG // STEP):
        fetch(a_hbm, held, sems, AGG // STEP, i).start()
    local_rows(
        1, acols, acount, a_hbm, (a0, a1), (b0, b1), out_ref, rh_ref, total, held, pc, sems
    )


LOCAL = [
    jax.ShapeDtypeStruct((2, 5, 3 * TILE, TILE), F32),
    jax.ShapeDtypeStruct((2, 3 * TILE, AGG * TILE), BF16),
]


def scratch():
    return [
        pltpu.VMEM((3 * AGG + 1, 3 * TILE, TILE), F32),
        pltpu.VMEM((AGG, SLOTS_A, TILE, TILE), BF16),
        pltpu.VMEM((3, ROWS, TILE, TILE), BF16),
    ]


def first_half(a_tiles, a_cols, a_count, p_tiles, p_cols, a0, b0):
    shape = jax.ShapeDtypeStruct((len(GROUPS[1]), AGG, TILE, TILE), BF16)
    return pl.pallas_call(
        first_kernel,
        out_shape=[shape, shape] + LOCAL,
        in_specs=[SMEM, SMEM, SMEM, HBM, HBM, VMEM, VMEM],
        out_specs=[VMEM] * 4,
        scratch_shapes=scratch()
        + [
            pltpu.VMEM((ROWS, SLOTS_P, TILE, TILE), BF16),
            pltpu.SemaphoreType.DMA((AGG // STEP,)),
            pltpu.SemaphoreType.DMA((ROWS // STEP,)),
        ],
        compiler_params=pltpu.CompilerParams(vmem_limit_bytes=40 * MIB),
        cost_estimate=pl.CostEstimate(
            flops=8 * 1024 * MIB, bytes_accessed=8 * MIB, transcendentals=0
        ),
    )(a_cols.T, a_count, p_cols.T, a_tiles, p_tiles, a0, b0)


def second_half(a_tiles, a_cols, a_count, a0, b0, a1, b1, local, rh):
    return pl.pallas_call(
        second_kernel,
        out_shape=LOCAL,
        in_specs=[SMEM, SMEM, HBM] + [VMEM] * 6,
        out_specs=[VMEM] * 2,
        scratch_shapes=scratch() + [pltpu.SemaphoreType.DMA((AGG // STEP,))],
        input_output_aliases={7: 0, 8: 1},
        compiler_params=pltpu.CompilerParams(vmem_limit_bytes=40 * MIB),
        cost_estimate=pl.CostEstimate(
            flops=8 * 1024 * MIB, bytes_accessed=8 * MIB, transcendentals=0
        ),
    )(a_cols.T, a_count, a_tiles, a0, b0, a1, b1, local, rh)


def tiles_of(chunk):
    return (0, 1, 2, 3) if chunk < 2 else (0, 1, 2)


def edge_tiles(group):
    below, above, at = [], [], 0
    for chunk in group:
        for t in tiles_of(chunk):
            for side in range(2):
                i = t if chunk < 2 else t + side
                column = 1 + chunk if side else -chunk
                if i == 0:
                    below.append((side, at, column + 4))
                if i == 3:
                    above.append((side, at, column + 1))
            at += 1
    below = [b for b in below if 2 <= b[2] < 7]
    above = [b for b in above if 0 <= b[2] < 5]
    return sorted(below, key=lambda b: b[2]), sorted(above, key=lambda b: b[2])


def finish_kernel(group, ha_ref, hb_ref, rh_ref, out_ref, tiles, *edge):
    device, sub, parity = place()
    for x, halo in enumerate((ha_ref, hb_ref)):
        side = x ^ (1 - parity)
        right = jnp.concatenate(
            [halo[at].reshape(AGG * TILE, TILE) for at in range(len(group))], axis=1
        )
        parts = jnp.dot(rh_ref[side], right, preferred_element_type=F32)
        first = 0
        for at, chunk in enumerate(group):
            part = parts[:, at * TILE : (at + 1) * TILE]
            part = part + out_ref[side, jnp.where(side == 0, 2 - chunk, 2 + chunk)]
            if chunk < 2:
                other = out_ref[1 - side, jnp.where(side == 0, 1 - chunk, 3 + chunk)]
                low = jnp.where(side == 0, part, other)
                high = jnp.where(side == 0, other, part)
                tiles[side, first] = low[:TILE]
                tiles[side, first + 1] = low[TILE : 2 * TILE] + high[:TILE]
                tiles[side, first + 2] = low[2 * TILE :] + high[TILE : 2 * TILE]
                tiles[side, first + 3] = high[2 * TILE :]
            else:
                for t in range(3):
                    tiles[side, first + t] = part[t * TILE : (t + 1) * TILE]
            first += len(tiles_of(chunk))
    if not edge:
        return
    below, above = edge_tiles(group)

    @pl.when(sub == 0)
    def _():
        for n, (side, at, _j) in enumerate(below):
            edge[0][n] = tiles[side, at].astype(BF16)

    @pl.when(sub == SUBS - 1)
    def _():
        for n, (side, at, _j) in enumerate(above):
            edge[0][n] = tiles[side, at].astype(BF16)


def last_edge_kernel(hb_ref, rh_ref, out_ref, edge):
    device, sub, parity = place()

    def one(side, t):
        rows = slice(t * TILE, (t + 1) * TILE)
        part = jnp.dot(
            rh_ref[side, rows, :], hb_ref[0].reshape(AGG * TILE, TILE), preferred_element_type=F32
        )
        edge[0] = (part + out_ref[side, 4 * side, rows]).astype(BF16)

    @pl.when(sub < SUBS - 1)
    def _():
        one(0, 0)

    @pl.when(sub == SUBS - 1)
    def _():
        one(1, 2)


def last_edge(hb, rh, local):
    return pl.pallas_call(
        last_edge_kernel,
        out_shape=jax.ShapeDtypeStruct((1, TILE, TILE), BF16),
        in_specs=[VMEM] * 3,
        out_specs=VMEM,
        compiler_params=pltpu.CompilerParams(vmem_limit_bytes=24 * MIB),
        cost_estimate=pl.CostEstimate(flops=64 * MIB, bytes_accessed=MIB, transcendentals=0),
    )(hb, rh, local)


def finish(group, with_edge, ha, hb, rh, local, *after):
    count = sum(len(tiles_of(c)) for c in group)
    shapes = [jax.ShapeDtypeStruct((2, count, TILE, TILE), F32)]
    if with_edge:
        edges = len(edge_tiles(group)[0])
        shapes.append(jax.ShapeDtypeStruct((edges, TILE, TILE), BF16))

    def kernel(*refs):
        finish_kernel(group, *refs[:4], *refs[4 + len(after) :])

    return pl.pallas_call(
        kernel,
        out_shape=shapes,
        in_specs=[VMEM] * (4 + len(after)),
        out_specs=[VMEM] * len(shapes),
        compiler_params=pltpu.CompilerParams(vmem_limit_bytes=24 * MIB),
        cost_estimate=pl.CostEstimate(
            flops=400 * MIB, bytes_accessed=6 * MIB, transcendentals=0
        ),
    )(ha, hb, rh, local, *after)


def split_kernel(groups, which, *refs):
    device, sub, parity = place()
    last = device >= (lax.axis_size("fine") - 1) * SUBS
    for d, target in zip(which, refs[2 * len(groups) :], strict=True):
        rows = pl.ds(pl.multiple_of((sub ^ d) * WIDE, WIDE), WIDE)
        base = 0
        for n_group, g in enumerate(groups):
            tiles, edge = refs[2 * n_group : 2 * n_group + 2]
            below, above = edge_tiles(GROUPS[g])
            for side in range(2):
                for i in range(tiles.shape[1]):
                    target[side, base + i] = tiles[side, i, rows, :].astype(BF16)

            @pl.when(sub == 0)
            def _():
                for n, (side, at, _j) in enumerate(below):
                    kept = jnp.where(last, 0.0, edge[n, rows, :].astype(F32))
                    target[side, base + at] = kept.astype(BF16)

            @pl.when(sub == SUBS - 1)
            def _():
                for n, (side, at, _j) in enumerate(above):
                    kept = jnp.where(device < SUBS, 0.0, edge[n, rows, :].astype(F32))
                    target[side, base + at] = kept.astype(BF16)

            base += tiles.shape[1]


def split(groups, which, tiles, edges, *after):
    count = sum(tiles[g].shape[1] for g in groups)
    shape = jax.ShapeDtypeStruct((2, count, WIDE, TILE), BF16)

    def kernel(*refs):
        split_kernel(groups, which, *refs[: 2 * len(groups)], *refs[2 * len(groups) + len(after) :])

    return pl.pallas_call(
        kernel,
        out_shape=[shape] * len(which),
        in_specs=[VMEM] * (2 * len(groups) + len(after)),
        out_specs=[VMEM] * len(which),
        compiler_params=pltpu.CompilerParams(vmem_limit_bytes=16 * MIB),
    )(*[x for g in groups for x in (tiles[g], edges[g])], *after)


def gather_kernel(kinds, *refs):
    parts, base, out_ref = refs[: len(kinds)], refs[len(kinds) : -1], refs[-1]
    device, sub, parity = place()
    out_ref[...] = base[0][...] if base else jnp.zeros_like(out_ref)
    for (d, groups), part in zip(kinds, parts, strict=True):
        first = 2 * (sub ^ d)
        at = 0
        for chunk in [c for g in groups for c in GROUPS[g]]:
            for t in tiles_of(chunk):
                for side in range(2):
                    column = 1 + chunk if side else -chunk
                    i = t if chunk < 2 else t + side
                    if 0 <= column - i + 4 < 7:
                        row = first + i - 1
                        row = jnp.where(row < 0, 7, jnp.where(row > 7, 0, row))
                        out_ref[row, column - i + 4] += part[side, at].astype(F32)
                at += 1


def gather_parts(kinds, parts, *base):
    def kernel(*refs):
        gather_kernel(kinds, *refs)

    return pl.pallas_call(
        kernel,
        out_shape=jax.ShapeDtypeStruct((8, 7, WIDE, TILE), F32),
        in_specs=[VMEM] * (len(parts) + len(base)),
        out_specs=VMEM,
        compiler_params=pltpu.CompilerParams(vmem_limit_bytes=16 * MIB),
    )(*parts, *base)


def shards(a_tiles, a_cols, a_count, p_tiles, p_cols):
    fines = lax.axis_size("fine")
    total = fines * SUBS
    both = ("fine", "sub")
    pairs_a = [(i, i ^ 1) for i in range(total)]
    pairs_b = [(i, (i - 1 + 2 * (i % 2)) % total) for i in range(total)]
    hop = []
    for q, other, step in ((0, 1, -1), (3, 2, 1)):
        down = [f * SUBS + q for f in range(fines)][::step]
        back = [f * SUBS + other for f in range(fines)][::-step]
        loop = down + back
        hop += list(zip(loop, loop[1:] + loop[:1], strict=True))

    a0, b0 = collapse(p_tiles, p_cols)
    halo = [(lax.ppermute(a0, both, pairs_a), lax.ppermute(b0, both, pairs_b))]
    a1, b1, local, rh = first_half(a_tiles, a_cols, a_count, p_tiles, p_cols, a0, b0)
    halo.append((lax.ppermute(a1, both, pairs_a), lax.ppermute(b1, both, pairs_b)))
    local, rh = second_half(a_tiles, a_cols, a_count, a0, b0, a1, b1, local, rh)
    tiles0, edge0 = finish(GROUPS[0], True, *halo[0], rh, local)
    edge1 = last_edge(halo[1][1], rh, local)
    (tiles1,) = finish(GROUPS[1], False, *halo[1], rh, local, edge1)
    tiles = [tiles0, tiles1]
    edges = [lax.ppermute(edge, both, hop) for edge in (edge0, edge1)]
    kinds, parts, first = [], [], []
    for groups, which in PLAN:
        cut = split(groups, which, tiles, edges, *first)
        first = cut if len(which) == 1 else []
        for d, part in zip(which, cut, strict=True):
            if d:
                part = lax.ppermute(part, "sub", [(i, i ^ d) for i in range(SUBS)])
            kinds.append((d, groups))
            parts.append(part)
    own = [n for n, (d, _) in enumerate(kinds) if d == 0]
    far = [n for n, (d, _) in enumerate(kinds) if d > 0]
    base = gather_parts([kinds[n] for n in own], [parts[n] for n in own])
    return gather_parts([kinds[n] for n in far], [parts[n] for n in far], base)


def solution(mesh):
    in_specs = (
        P(("fine", "sub"), None, None, None),
        P(("fine", "sub"), None),
        P(("fine", "sub")),
        P(("fine", "sub"), None, None, None),
        P(("fine", "sub"), None),
    )
    out_specs = P("fine", None, "sub", None)
    return jax.shard_map(shards, mesh=mesh, in_specs=in_specs, out_specs=out_specs, check_vma=False)
```
